32 devices in a mesh: groups: 2 (over x), dom: 16 (over z, y, core).
Axes of the slice: x: 2, y: 2, z: 4, core: 2. Of those that a mesh axis runs over, the one named last changes fastest.
Arguments:
- features: bfloat16 [16384, 2048], P(('groups', 'dom')), parts along dimension 0, may hold values from -6 to 6
- cotangent: bfloat16 [16384, 2048], P(('groups', 'dom')), parts along dimension 0, may hold values from -0.5 to 0.5
- positions: bfloat16 [3, 16384], P(None, ('groups', 'dom')), parts along dimension 1, may hold values from 0 to 1
- value_weight: bfloat16 [4, 128, 128], replicated, may hold values from -0.5 to 0.5
- query_weight: bfloat16 [128, 128], replicated, may hold values from -0.5 to 0.5
- key_weight: bfloat16 [128, 128], replicated, may hold values from -0.5 to 0.5
- ghost_index: int32 [32, 2, 256], P(('groups', 'dom')), parts along dimension 0, may hold values from 0 to 511, as said below
- tile_pairs: int32 [32, 3, 8, 2], P(('groups', 'dom')), parts along dimension 0, may hold values from 0 to 3, as said below
- tile_counts: int32 [32, 3], P(('groups', 'dom')), parts along dimension 0, may hold values from 1 to 8, as said below
Outputs:
- feat_adjoint: bfloat16 [16384, 2048], P(('groups', 'dom')), parts along dimension 0
- forces: float32 [3, 16384], P(None, ('groups', 'dom')), parts along dimension 1
The draws below stay inside these ranges and needn't reach their ends.
There are 2 independent parts, one for each index of `groups`. The reference program is written for one: setup_inputs(seed, part) draws one part's arguments, and reference() takes and returns one part's arrays. A program takes and returns all parts, laid end to end along the dimension named above; an argument that names none is the same for every part. Nothing has to cross between parts.
Inputs may be any that keep to these rules, and one draw needn't show every extreme that they name: Each list ghost_index[d, k, :] names 256 different local atoms of domain d. tile_pairs[d, 0, :] holds different pairs (a, b) with a <= b; for k >= 1, tile_pairs[d, k, :] holds all pairs with a < 4 and b < 2, each once. Only the first tile_counts[d, k] slots of tile_pairs[d, k] are used; in every round some domain uses all 8.
All inputs are finite; a program needn't handle non-finite values.
Results may differ from the reference program's by a relative error of at most 0.0064.
Values may be sent and summed in bfloat16 or wider, within the bound.
A program may use at most 128 MiB of HBM per device.

```python
import jax
import jax.numpy as jnp
from jax import lax

CHANNELS = 128
FEAT = 2048
KEY_WIDTH = 128
TILE = 128
ATOMS_DEV = 512
GHOSTS = 256
ROUNDS = 2
SLOTS = 8
DOMAINS = 16
ATOMS = 8192


def draw_ghost_index(key, part):
    subkeys = jax.random.split(key, DOMAINS * ROUNDS)
    chosen = jax.vmap(lambda subkey: jax.random.permutation(subkey, ATOMS_DEV)[:GHOSTS])(subkeys)
    return chosen.reshape(DOMAINS, ROUNDS, GHOSTS).astype(jnp.int32)


def draw_tile_pairs(key, part):
    own_tiles = ATOMS_DEV // TILE
    ghost_tiles = GHOSTS // TILE
    square = own_tiles * own_tiles
    entries = jnp.arange(square, dtype=jnp.int32)
    first_tile = entries // own_tiles
    second_tile = entries % own_tiles
    invalid = (first_tile > second_tile).astype(jnp.int32)
    key_intra, key_cross = jax.random.split(jax.random.fold_in(key, 11))
    scores = jax.random.randint(key_intra, (DOMAINS, square), 0, 1 << 20) + invalid[None, :] * (1 << 22)
    ordering = jnp.argsort(scores, axis=1, stable=True)[:, :SLOTS]
    intra = jnp.stack([first_tile[ordering], second_tile[ordering]], axis=-1)
    cross_total = own_tiles * ghost_tiles
    cross_keys = jax.random.split(key_cross, DOMAINS * ROUNDS)
    shuffled = jax.vmap(lambda subkey: jax.random.permutation(subkey, cross_total)[:SLOTS])(cross_keys).reshape(DOMAINS, ROUNDS, SLOTS)
    cross = jnp.stack([shuffled // ghost_tiles, shuffled % ghost_tiles], axis=-1)
    return jnp.concatenate([intra[:, None], cross], axis=1).astype(jnp.int32)


def draw_tile_counts(key, part):
    key_one, key_two, key_hot = jax.random.split(jax.random.fold_in(key, 23), 3)
    first_draw = jax.random.randint(key_one, (DOMAINS, ROUNDS + 1), 0, SLOTS)
    second_draw = jax.random.randint(key_two, (DOMAINS, ROUNDS + 1), 0, SLOTS)
    counts = jnp.minimum(first_draw, second_draw) + 1
    busiest = jax.random.randint(key_hot, (ROUNDS + 1,), 0, DOMAINS)
    domain_ids = jnp.arange(DOMAINS, dtype=jnp.int32)[:, None]
    return jnp.where(domain_ids == busiest[None, :], SLOTS, counts).astype(jnp.int32)


def block_scale(rng, dims, shards, low, top_value):
    factor_of, own = 1.0, jax.random.fold_in(rng, 6)
    for dim, shards_of in shards:
        heights = jnp.exp(jax.random.uniform(jax.random.fold_in(own, dim), (shards_of,), jnp.float32, low / len(shards), top_value / len(shards)))
        factor_of = factor_of * jnp.repeat(heights, dims[dim] // shards_of).reshape([-1 if axis == dim else 1 for axis in range(len(dims))])
    return factor_of


def scatter_about(rng, shape, deviation, limit, shards=(), kind=jnp.bfloat16):
    values = deviation * jax.random.normal(rng, shape, jnp.float32)
    if shards:
        values = values * block_scale(rng, shape, shards, -0.22, 0.18)
    return jnp.clip(values, -limit, limit).astype(kind)


def setup_inputs(seed: int = 0, part: int = 0) -> dict:
    seeds = jax.random.split(jax.random.key(seed), 10)
    part_keys = jax.random.split(jax.random.fold_in(seeds[9], part), 10)
    return {
        "features": scatter_about(part_keys[0], (ATOMS, FEAT), 1.0, 6.0, ((0, 16),)),
        "cotangent": scatter_about(part_keys[1], (ATOMS, FEAT), (4.0 * (16 * CHANNELS) ** -0.5), 0.5, ((0, 16),)),
        "positions": jnp.clip(1.0 * jax.random.uniform(part_keys[2], (3, ATOMS), jnp.float32) ** block_scale(part_keys[2], (3, ATOMS), ((1, 16),), -0.2, 0.2), 0.0, 1.0).astype(jnp.bfloat16),
        "value_weight": scatter_about(seeds[3], (4, CHANNELS, CHANNELS), CHANNELS ** -0.5, 0.5),
        "query_weight": scatter_about(seeds[4], (CHANNELS, KEY_WIDTH), CHANNELS ** -0.5, 0.5),
        "key_weight": scatter_about(seeds[5], (CHANNELS, KEY_WIDTH), CHANNELS ** -0.5, 0.5),
        "ghost_index": draw_ghost_index(jax.random.fold_in(jax.random.fold_in(seeds[9], part), 71), part),
        "tile_pairs": draw_tile_pairs(jax.random.fold_in(jax.random.fold_in(seeds[9], part), 71), part),
        "tile_counts": draw_tile_counts(jax.random.fold_in(jax.random.fold_in(seeds[9], part), 71), part),
    }


CUTOFF_SQ = 9.0


def contract_rows(left_op, right_op):
    return lax.dot_general(left_op, right_op, (((1,), (1,)), ((), ())), preferred_element_type=jnp.float32)


def contract_cols(left_op, right_op):
    return lax.dot_general(left_op, right_op, (((0,), (0,)), ((), ())), preferred_element_type=jnp.float32)


def project(feats, weight_set, backward):
    count_rows = feats.shape[0]
    chan_width = weight_set.shape[1]
    pieces = []
    for degree in range(4):
        low_col = degree * degree * chan_width
        high_col = (degree + 1) * (degree + 1) * chan_width
        block_rows = feats[:, low_col:high_col].reshape(count_rows * (2 * degree + 1), chan_width)
        if backward:
            mixed = contract_rows(block_rows, weight_set[degree])
        else:
            mixed = jnp.dot(block_rows, weight_set[degree], preferred_element_type=jnp.float32)
        pieces.append(mixed.reshape(count_rows, high_col - low_col))
    return jnp.concatenate(pieces, axis=1)


def tile_terms(own_tile, other_tile, diagonal, score_scale):
    cot_own, val_own, qry_own, key_own, pos_own = own_tile
    cot_oth, val_oth, qry_oth, key_oth, pos_oth = other_tile
    grad_in = contract_rows(cot_own, val_oth)
    grad_out = contract_rows(val_own, cot_oth)
    score_in = score_scale * contract_rows(qry_own, key_oth)
    score_out = score_scale * contract_rows(key_own, qry_oth)
    offsets = pos_own[:, :, None] - pos_oth[:, None, :]
    dist_sq = jnp.sum(offsets * offsets, axis=0)
    inside = jnp.maximum(1.0 - dist_sq / CUTOFF_SQ, 0.0)
    smooth = inside * inside
    smooth_slope = (-2.0 / CUTOFF_SQ) * inside
    row_ids = lax.broadcasted_iota(jnp.int32, dist_sq.shape, 0)
    col_ids = lax.broadcasted_iota(jnp.int32, dist_sq.shape, 1)
    keep_mask = jnp.where(jnp.logical_or(jnp.logical_not(diagonal), row_ids < col_ids), 1.0, 0.0).astype(jnp.float32)
    gate_in = jax.nn.sigmoid(score_in)
    gate_out = jax.nn.sigmoid(score_out)
    masked = smooth * keep_mask
    weight_in = (masked * gate_in).astype(jnp.bfloat16)
    weight_out = (masked * gate_out).astype(jnp.bfloat16)
    zgrad_in = (grad_in * masked * gate_in * (1.0 - gate_in)).astype(jnp.bfloat16)
    zgrad_out = (grad_out * masked * gate_out * (1.0 - gate_out)).astype(jnp.bfloat16)
    rho_grad = (grad_in * gate_in + grad_out * gate_out) * smooth_slope * keep_mask
    upd_own = jnp.dot(weight_out, cot_oth, preferred_element_type=jnp.float32)
    upd_oth = contract_cols(weight_in, cot_own)
    gq_own = score_scale * jnp.dot(zgrad_in, key_oth, preferred_element_type=jnp.float32)
    gk_own = score_scale * jnp.dot(zgrad_out, qry_oth, preferred_element_type=jnp.float32)
    gq_oth = score_scale * contract_cols(zgrad_out, key_own)
    gk_oth = score_scale * contract_cols(zgrad_in, qry_own)
    push_term = 2.0 * rho_grad[None] * offsets
    gp_own = jnp.sum(push_term, axis=2)
    gp_oth = -jnp.sum(push_term, axis=1)
    return (upd_own, gq_own, gk_own, gp_own), (upd_oth, gq_oth, gk_oth, gp_oth)


def bump(target, addend, first_row, along_dim):
    current = lax.dynamic_slice_in_dim(target, first_row, addend.shape[along_dim], along_dim)
    return lax.dynamic_update_slice_in_dim(target, current + addend, first_row, along_dim)


def add_rows(sums, terms, first_row):
    return (bump(sums[0], terms[0], first_row, 0), bump(sums[1], terms[1], first_row, 0), bump(sums[2], terms[2], first_row, 0), bump(sums[3], terms[3], first_row, 1))


def cut_tile(side, first_row):
    return (lax.dynamic_slice_in_dim(side[0], first_row, TILE, 0), lax.dynamic_slice_in_dim(side[1], first_row, TILE, 0), lax.dynamic_slice_in_dim(side[2], first_row, TILE, 0), lax.dynamic_slice_in_dim(side[3], first_row, TILE, 0), lax.dynamic_slice_in_dim(side[4], first_row, TILE, 1))


def run_round(own_side, other_side, own_sums, other_sums, pair_list, pair_count, is_intra, score_scale):
    def visit_pair(slot_index, carried):
        sums_a, sums_b = carried
        tile_a = pair_list[slot_index, 0]
        tile_b = pair_list[slot_index, 1]
        start_a = tile_a * TILE
        start_b = tile_b * TILE
        diagonal = jnp.logical_and(is_intra, tile_a == tile_b)
        terms_a, terms_b = tile_terms(cut_tile(own_side, start_a), cut_tile(other_side, start_b), diagonal, score_scale)
        return add_rows(sums_a, terms_a, start_a), add_rows(sums_b, terms_b, start_b)
    return lax.fori_loop(0, pair_count, visit_pair, (own_sums, other_sums))


def empty_sums(count_rows, feat_width, key_width):
    return (jnp.zeros((count_rows, feat_width), jnp.float32), jnp.zeros((count_rows, key_width), jnp.float32), jnp.zeros((count_rows, key_width), jnp.float32), jnp.zeros((3, count_rows), jnp.float32))


def reference(features, cotangent, positions, value_weight, query_weight, key_weight, ghost_index, tile_pairs, tile_counts):
    domains = ghost_index.shape[0]
    rounds = ghost_index.shape[1]
    chan_width = value_weight.shape[1]
    key_width = query_weight.shape[1]
    feat_width = features.shape[1]
    atoms_dev = features.shape[0] // domains
    score_scale = key_width ** -0.5
    values = project(features, value_weight, False).astype(jnp.bfloat16)
    queries = jnp.dot(features[:, :chan_width], query_weight, preferred_element_type=jnp.float32).astype(jnp.bfloat16)
    keys_all = jnp.dot(features[:, :chan_width], key_weight, preferred_element_type=jnp.float32).astype(jnp.bfloat16)
    points = positions.astype(jnp.float32)
    cot_dom = cotangent.reshape(domains, atoms_dev, feat_width)
    val_dom = values.reshape(domains, atoms_dev, feat_width)
    qry_dom = queries.reshape(domains, atoms_dev, key_width)
    key_dom = keys_all.reshape(domains, atoms_dev, key_width)
    pts_dom = points.reshape(3, domains, atoms_dev).transpose(1, 0, 2)

    def evaluate(domain):
        own_side = (cot_dom[domain], val_dom[domain], qry_dom[domain], key_dom[domain], pts_dom[domain])
        own_sums, self_sums = run_round(own_side, own_side, empty_sums(atoms_dev, feat_width, key_width), empty_sums(atoms_dev, feat_width, key_width), tile_pairs[domain, 0], tile_counts[domain, 0], True, score_scale)
        own_sums = tuple(left_sum + right_sum for left_sum, right_sum in zip(own_sums, self_sums))
        packets = []
        for distance in range(1, rounds + 1):
            source = (domain + distance) % domains
            picked = ghost_index[source, distance - 1]
            shift_vector = jnp.array([distance, 0, 0], jnp.float32)[:, None]
            other_side = (cot_dom[source][picked], val_dom[source][picked], qry_dom[source][picked], key_dom[source][picked], pts_dom[source][:, picked] + shift_vector)
            own_sums, ghost_sums = run_round(own_side, other_side, own_sums, empty_sums(picked.shape[0], feat_width, key_width), tile_pairs[domain, distance], tile_counts[domain, distance], False, score_scale)
            packets.append(tuple(member.astype(jnp.bfloat16) for member in ghost_sums))
        return own_sums, tuple(packets)

    totals, packets = lax.map(evaluate, jnp.arange(domains, dtype=jnp.int32))
    sum_u, sum_q, sum_k, sum_p = totals
    for distance in range(1, rounds + 1):
        moved = tuple(jnp.roll(member, distance, axis=0) for member in packets[distance - 1])
        picked = ghost_index[:, distance - 1]
        sum_u = jax.vmap(lambda target, where_rows, addend: target.at[where_rows].add(addend.astype(jnp.float32)))(sum_u, picked, moved[0])
        sum_q = jax.vmap(lambda target, where_rows, addend: target.at[where_rows].add(addend.astype(jnp.float32)))(sum_q, picked, moved[1])
        sum_k = jax.vmap(lambda target, where_rows, addend: target.at[where_rows].add(addend.astype(jnp.float32)))(sum_k, picked, moved[2])
        sum_p = jax.vmap(lambda target, where_rows, addend: target.at[:, where_rows].add(addend.astype(jnp.float32)))(sum_p, picked, moved[3])
    total_u = sum_u.reshape(domains * atoms_dev, feat_width).astype(jnp.bfloat16)
    total_q = sum_q.reshape(domains * atoms_dev, key_width).astype(jnp.bfloat16)
    total_k = sum_k.reshape(domains * atoms_dev, key_width).astype(jnp.bfloat16)
    backward = project(total_u, value_weight, True)
    scalar_part = contract_rows(total_q, query_weight) + contract_rows(total_k, key_weight)
    feat_adjoint = backward.at[:, :chan_width].add(scalar_part).astype(jnp.bfloat16)
    forces = (-sum_p).transpose(1, 0, 2).reshape(3, domains * atoms_dev)
    return feat_adjoint, forces
```

```python
import functools

import jax
import jax.numpy as jnp
from jax import lax
from jax.experimental import pallas as pl
from jax.experimental.pallas import tpu as pltpu
from jax.sharding import PartitionSpec as P

TILE = 128
CUTOFF_SQ = 9.0
CHUNKS = 2
VMEM_BYTES = 48 * 2**20
F32 = jnp.float32
BF16 = jnp.bfloat16


def dot_nt(left, right):
    return lax.dot_general(left, right, (((1,), (1,)), ((), ())), preferred_element_type=F32)


def dot_tn(left, right):
    return lax.dot_general(left, right, (((0,), (0,)), ((), ())), preferred_element_type=F32)


def dot_nn(left, right):
    return lax.dot_general(left, right, (((1,), (0,)), ((), ())), preferred_element_type=F32)


def project_kernel(feat_ref, vw_ref, qw_ref, kw_ref, val_ref, qry_ref, key_ref):
    chan = vw_ref.shape[1]
    for comp in range(16):
        cols = slice(comp * chan, (comp + 1) * chan)
        degree = int(comp**0.5)
        val_ref[:, cols] = dot_nn(feat_ref[:, cols], vw_ref[degree]).astype(BF16)
    scalars = feat_ref[:, :chan]
    qry_ref[...] = dot_nn(scalars, qw_ref[...]).astype(BF16)
    key_ref[...] = dot_nn(scalars, kw_ref[...]).astype(BF16)


def final_kernel(u_ref, q_ref, k_ref, vw_ref, qw_ref, kw_ref, out_ref):
    chan = vw_ref.shape[1]
    for comp in range(16):
        cols = slice(comp * chan, (comp + 1) * chan)
        degree = int(comp**0.5)
        mixed = dot_nt(u_ref[:, cols].astype(BF16), vw_ref[degree])
        if comp == 0:
            mixed += dot_nt(q_ref[...].astype(BF16), qw_ref[...])
            mixed += dot_nt(k_ref[...].astype(BF16), kw_ref[...])
        out_ref[:, cols] = mixed.astype(BF16)


def block_kernel(chunks, own, first, scale, *refs):
    val_ref, key_ref, pt_ref, row_ref = refs[:4]
    refs = refs[4:]
    cot_refs, refs = refs[:chunks], refs[chunks:]
    qry_ref, ps_ref, col_ref = refs[:3]
    refs = refs[3:]
    if not first:
        u_in, k_in, p_in = refs[:3]
        refs = refs[3:]
    u_out, k_out, p_out, q_src, p_src = refs
    atoms = val_ref.shape[0]
    step = TILE * 2
    rows_chunk = atoms // chunks
    q_src[...] = jnp.zeros_like(q_src)
    p_src[...] = jnp.zeros_like(p_src)
    nmask = row_ref.shape[1]
    for c in range(chunks):
        src = slice(c * rows_chunk, (c + 1) * rows_chunk)
        cot = cot_refs[c]
        for r in range(atoms // step):
            tgt = slice(r * step, (r + 1) * step)
            grad = dot_nt(val_ref[tgt, :], cot[...])
            score = scale * dot_nt(key_ref[tgt, :], qry_ref[src, :])
            diffs = [pt_ref[tgt, x : x + 1] - ps_ref[x : x + 1, src] for x in range(3)]
            dist = diffs[0] * diffs[0] + diffs[1] * diffs[1] + diffs[2] * diffs[2]
            inside = jnp.maximum(1.0 - dist * (1.0 / CUTOFF_SQ), 0.0)
            keep = row_ref[tgt, 0:1] * col_ref[0:1, src]
            for b in range(1, nmask):
                keep += row_ref[tgt, b : b + 1] * col_ref[b : b + 1, src]
            if own:
                row_id = lax.broadcasted_iota(jnp.int32, keep.shape, 0) + r * step
                col_id = lax.broadcasted_iota(jnp.int32, keep.shape, 1) + c * rows_chunk
                keep = jnp.where(row_id == col_id, 0.0, keep)
            gate = jax.nn.sigmoid(score)
            kept = keep * inside
            half = kept * gate
            weight = half * inside
            zgrad = (grad * weight * (1.0 - gate)).astype(BF16)
            push = (-4.0 / CUTOFF_SQ) * grad * half
            weight = weight.astype(BF16)
            upd = dot_nn(weight, cot[...])
            kup = scale * dot_nn(zgrad, qry_ref[src, :])
            fresh = first and c == 0
            base_u, base_k, base_p = (u_out, k_out, p_out) if c else (None,) * 3
            if c == 0 and not first:
                base_u, base_k, base_p = u_in, k_in, p_in
            if fresh:
                u_out[tgt, :] = upd
                k_out[tgt, :] = kup
            else:
                u_out[tgt, :] = base_u[tgt, :] + upd
                k_out[tgt, :] = base_k[tgt, :] + kup
            q_src[src, :] += scale * dot_tn(zgrad, key_ref[tgt, :])
            for x in range(3):
                term = push * diffs[x]
                across = jnp.sum(term, axis=1, keepdims=True)
                if fresh:
                    p_out[tgt, x : x + 1] = across
                else:
                    p_out[tgt, x : x + 1] = base_p[tgt, x : x + 1] + across
                p_src[x : x + 1, src] -= jnp.sum(term, axis=0, keepdims=True)


def whole(n):
    return [pl.BlockSpec(memory_space=pltpu.VMEM)] * n


def run_block(own_side, row_mask, cots, block_small, sums, own, scale):
    values, keys, pt = own_side
    qry, ps, col_mask = block_small
    atoms, feat = values.shape
    width = keys.shape[1]
    first = sums is None
    args = [values, keys, pt, row_mask, *cots, qry, ps, col_mask]
    if not first:
        args += list(sums)
    out = [
        jax.ShapeDtypeStruct((atoms, feat), F32),
        jax.ShapeDtypeStruct((atoms, width), F32),
        jax.ShapeDtypeStruct((atoms, 8), F32),
        jax.ShapeDtypeStruct((atoms, width), F32),
        jax.ShapeDtypeStruct((8, atoms), F32),
    ]
    u, k, p, qs, psrc = pl.pallas_call(
        functools.partial(block_kernel, len(cots), own, first, scale),
        out_shape=out,
        in_specs=whole(len(args)),
        out_specs=whole(5),
        compiler_params=pltpu.CompilerParams(vmem_limit_bytes=VMEM_BYTES),
        cost_estimate=pl.CostEstimate(
            flops=4 * atoms * atoms * feat, bytes_accessed=14 * 2**20, transcendentals=atoms * atoms
        ),
    )(*args)
    return (u, k, p), (qs, psrc)


def shards(
    features, cotangent, positions, value_weight, query_weight, key_weight, ghost_index, tile_pairs, tile_counts
):
    atoms, feat = features.shape
    chan = value_weight.shape[1]
    width = query_weight.shape[1]
    scale = width ** (-0.5)
    slots = tile_pairs.shape[2]
    tiles = atoms // TILE
    gtiles = ghost_index.shape[2] // TILE
    domains = lax.axis_size("dom")
    me = lax.axis_index("dom")
    core = me % 2
    side = (me // 2) % 2

    def bit(i, b):
        return (i >> b) & 1

    def send(block, rule):
        return lax.ppermute(block, "dom", [(i, rule(i) % domains) for i in range(domains)])

    across = lambda i: i ^ 2
    along = lambda i: i + 4 if bit(i, 1) == 0 else i - 4
    twin = lambda i: i ^ 1
    back_far = lambda i: i - 2 if bit(i, 1) == 0 else i + 2
    back_near = lambda i: i - 1 if bit(i, 0) == 0 else i + 1

    values, queries, keys = pl.pallas_call(
        project_kernel,
        out_shape=[
            jax.ShapeDtypeStruct((atoms, feat), BF16),
            jax.ShapeDtypeStruct((atoms, width), BF16),
            jax.ShapeDtypeStruct((atoms, width), BF16),
        ],
        in_specs=whole(4),
        out_specs=whole(3),
        compiler_params=pltpu.CompilerParams(vmem_limit_bytes=VMEM_BYTES),
    )(features, value_weight, query_weight, key_weight)

    used = jnp.arange(slots, dtype=jnp.int32)[None, :] < tile_counts[0][:, None]
    ids = jnp.arange(tiles, dtype=jnp.int32)
    hit_a = tile_pairs[0, :, :, 0, None] == ids
    hit_b = tile_pairs[0, :, :, 1, None] == ids
    active = jnp.sum(
        (hit_a[:, :, :, None] & hit_b[:, :, None, :] & used[:, :, None, None]).astype(F32), axis=1
    )
    intra = jnp.maximum(active[0], active[0].T)
    atom_ids = jnp.arange(atoms, dtype=jnp.int32)
    listed = ghost_index[0].reshape(2, gtiles, TILE)
    ghost_rows = jnp.sum((listed[:, :, :, None] == atom_ids).astype(F32), axis=2)
    act_rows = jnp.repeat(active[1:, :, :gtiles].transpose(0, 2, 1), TILE, axis=2)

    small = jnp.concatenate(
        [
            queries,
            positions.reshape(3 * atoms // 128, 128),
            jnp.zeros((4, 128), BF16),
            ghost_rows.astype(BF16).reshape(-1, 128),
            act_rows.astype(BF16).reshape(-1, 128),
        ],
        axis=0,
    )
    small_1 = send(small, across)
    small_0 = send(small, twin)
    small_3 = send(small_1, along)
    straight = (side == 0) == (core == 0)
    small_p = send(jnp.where(straight, small_1, small_3), twin)

    rows = atoms // CHUNKS
    cut = lambda c: cotangent[c * rows : (c + 1) * rows]
    cot_0 = send(cotangent, twin)
    cot_1, cot_3, cot_p = [], [], []
    for c in range(CHUNKS):
        cot_1.append(send(cut(c), across))
        cot_3.append(send(cot_1[c], along))
        cot_p.append(send(jnp.where(straight, cot_1[c], cot_3[c]), twin))

    points = positions.astype(F32)
    pt = jnp.pad(points.T, ((0, 0), (0, 5)))
    own_side = (values, keys, pt)

    def unpack(pack, step, forward):
        qry = pack[:atoms]
        pos = pack[atoms : atoms + 3 * atoms // 128].reshape(3, atoms).astype(F32)
        shift = jnp.where(forward, step, -step).astype(F32)
        ps = jnp.pad(pos + jnp.array([1.0, 0.0, 0.0], F32)[:, None] * shift, ((0, 5), (0, 0)))
        marks = pack[atoms + 3 * atoms // 128 + 4 :].astype(F32).reshape(2, 2, gtiles, atoms)[:, step - 1]
        col = jnp.where(forward, marks[0], marks[1])
        row = jnp.where(forward, act_rows[step - 1], ghost_rows[step - 1])
        return (qry, ps, jnp.pad(col, ((0, 8 - gtiles), (0, 0)))), row.T

    one_hot = jnp.repeat(jnp.eye(tiles, dtype=F32), TILE, axis=1)
    own_small = (queries, jnp.pad(points, ((0, 5), (0, 0))), jnp.pad(one_hot, ((0, 8 - tiles), (0, 0))))
    own_rows = jnp.repeat(intra, TILE, axis=0)

    def pack_back(src):
        qs, ps = src
        return jnp.concatenate([qs, ps[:4].reshape(-1, 128)], axis=0).astype(BF16)

    sums, own_src = run_block(own_side, own_rows, [cotangent], own_small, None, True, scale)
    plan = [
        (small_0, [cot_0], 1, core == 0, twin),
        (small_1, cot_1, 2, side == 0, across),
        (small_3, cot_3, 2, side == 1, back_far),
        (small_p, cot_p, 1, core == 1, back_near),
    ]
    returned = []
    for pack, cots, step, forward, back in plan:
        block_small, row = unpack(pack, step, forward)
        sums, src = run_block(own_side, row, cots, block_small, sums, False, scale)
        returned.append(send(pack_back(src), back))
    sum_u, sum_k, sum_p = sums
    sum_q, p_src = own_src
    sum_p = sum_p[:, :3].T + p_src[:3]
    for pack in returned:
        sum_q = sum_q + pack[:atoms].astype(F32)
        sum_p = sum_p + pack[atoms:].astype(F32).reshape(4, atoms)[:3]
    adjoint = pl.pallas_call(
        final_kernel,
        out_shape=jax.ShapeDtypeStruct((atoms, feat), BF16),
        in_specs=whole(6),
        out_specs=pl.BlockSpec(memory_space=pltpu.VMEM),
        compiler_params=pltpu.CompilerParams(vmem_limit_bytes=VMEM_BYTES),
    )(sum_u, sum_q, sum_k, value_weight, query_weight, key_weight)
    return adjoint, -sum_p


def solution(mesh):
    both = ("groups", "dom")
    placed = (
        P(both, None),
        P(both, None),
        P(None, both),
        P(),
        P(),
        P(),
        P(both, None, None),
        P(both, None, None, None),
        P(both, None),
    )
    return jax.shard_map(
        shards, mesh=mesh, in_specs=placed, out_specs=(P(both, None), P(None, both)), check_vma=False
    )
```

```python
import functools

import jax
import jax.numpy as jnp
from jax import lax
from jax.experimental import pallas as pl
from jax.experimental.pallas import tpu as pltpu
from jax.sharding import PartitionSpec as P

TILE = 128
CUTOFF_SQ = 9.0
CHUNKS = 4
VMEM_BYTES = 48 * 2**20
F32 = jnp.float32
BF16 = jnp.bfloat16


def dot_nt(left, right):
    return lax.dot_general(left, right, (((1,), (1,)), ((), ())), preferred_element_type=F32)


def dot_tn(left, right):
    return lax.dot_general(left, right, (((0,), (0,)), ((), ())), preferred_element_type=F32)


def dot_nn(left, right):
    return lax.dot_general(left, right, (((1,), (0,)), ((), ())), preferred_element_type=F32)


def whole(n):
    return [pl.BlockSpec(memory_space=pltpu.VMEM)] * n


def block_terms(tables, acc, tgt, src, own, fwd, step, scale, cot_ref, qry_ref, meta_ref, slot):
    val_ref, key_ref, turn_ref = tables
    u_acc, k_acc, p_acc, q_src, p_src = acc
    cot = cot_ref[src, :]
    qry = qry_ref[src, :]
    grad = dot_nt(val_ref[tgt, :], cot)
    score = scale * dot_nt(key_ref[tgt, :], qry)
    keys = key_ref[tgt, :]
    turn = turn_ref[tgt, :]
    meta = meta_ref[:, src].astype(F32)
    if own:
        shift = 0.0
        keep = turn[:, 11:12] * meta[11:12]
        for b in range(1, 4):
            keep += turn[:, 11 + b : 12 + b] * meta[11 + b : 12 + b]
        row_id = lax.broadcasted_iota(jnp.int32, keep.shape, 0) + tgt.start
        col_id = lax.broadcasted_iota(jnp.int32, keep.shape, 1) + src.start
        keep = jnp.where(row_id == col_id, 0.0, keep)
    else:
        shift = jnp.where(fwd, float(step), -float(step))
        lent, used = 1 + 2 * step, 5 + 2 * step
        keep = None
        for b in range(2):
            row = jnp.where(fwd, turn[:, used + b : used + b + 1], turn[:, lent + b : lent + b + 1])
            col = jnp.where(fwd, meta[lent + b : lent + b + 1], meta[used + b : used + b + 1])
            keep = row * col if keep is None else keep + row * col
    diffs = [turn[:, x : x + 1] - (meta[x : x + 1] + (shift if x == 0 else 0.0)) for x in range(3)]
    dist = diffs[0] * diffs[0] + diffs[1] * diffs[1] + diffs[2] * diffs[2]
    inside = jnp.maximum(1.0 - dist * (1.0 / CUTOFF_SQ), 0.0)
    gate = jax.nn.sigmoid(score)
    half = keep * inside * gate
    weight = half * inside
    zgrad = (grad * weight * (1.0 - gate)).astype(BF16)
    push = (-4.0 / CUTOFF_SQ) * grad * half
    u_acc[tgt, :] += dot_nn(weight.astype(BF16), cot)
    k_acc[tgt, :] += scale * dot_nn(zgrad, qry)
    q_src[slot, src, :] += scale * dot_tn(zgrad, keys)
    for x in range(3):
        term = push * diffs[x]
        p_acc[tgt, x : x + 1] += jnp.sum(term, axis=1, keepdims=True)
        p_src[slot, x : x + 1, src] -= jnp.sum(term, axis=0, keepdims=True)


def layer_kernel(
    domains, scale,
    feat_ref, cot_ref, meta_ref, turn_ref, vw_ref, qw_ref, kw_ref,
    out_ref, force_ref,
    val_ref, qry_ref, key_ref, cots, qrys, metas,
    u_acc, k_acc, p_acc, q_src, p_src, q_out, p_out, q_back, p_back,
    send_sem, recv_sem,
):
    atoms = feat_ref.shape[0]
    chan = vw_ref.shape[1]
    rows = atoms // CHUNKS
    me = lax.axis_index("dom")
    core = lax.rem(me, 2)
    side = lax.rem(me // 2, 2)
    wrap = lambda i: lax.rem(i + domains, domains)
    twin = me + 1 - 2 * core
    across = me + 2 - 4 * side
    along = wrap(me + 4 - 8 * side)
    behind = wrap(me - 4 + 8 * side)
    far = wrap(me - 2 + 4 * side)
    near = wrap(me - 1 + 2 * core)
    straight = side == core

    barrier = pltpu.get_barrier_semaphore()
    for peer in (twin, across, along, behind, far, near):
        pl.semaphore_signal(
            barrier, inc=1, device_id={"dom": peer}, device_id_type=pl.DeviceIdType.MESH
        )

    def copy(src, dst, index, peer):
        return pltpu.make_async_remote_copy(
            src_ref=src,
            dst_ref=dst,
            send_sem=send_sem.at[index],
            recv_sem=recv_sem.at[index],
            device_id={"dom": peer},
            device_id_type=pl.DeviceIdType.MESH,
        )

    small = lambda q, m, slot, peer: (
        copy(q, qrys.at[slot], 2 * slot, peer),
        copy(m, metas.at[slot], 2 * slot + 1, peer),
    )
    piece = lambda ref, c: ref.at[c * rows : (c + 1) * rows]
    part = lambda slot, c: cots.at[slot, c * rows : (c + 1) * rows]
    big = lambda src, slot, c, peer: copy(piece(src, c), part(slot, c), 8 + slot * CHUNKS + c, peer)

    scalars = feat_ref[:, :chan]
    qry_ref[...] = dot_nn(scalars, qw_ref[...]).astype(BF16)
    pl.semaphore_wait(barrier, 6)
    sent = []

    def begin(copies):
        for item in copies:
            item.start()
            sent.append(item)

    small_1 = small(qry_ref, meta_ref, 1, across)
    small_0 = small(qry_ref, meta_ref, 0, twin)
    begin(small_1)
    big_1 = [big(cot_ref, 1, c, across) for c in range(CHUNKS)]
    begin(big_1)
    begin(small_0)
    big_0 = [big(cot_ref, 0, c, twin) for c in range(CHUNKS)]
    begin(big_0)

    key_ref[...] = dot_nn(scalars, kw_ref[...]).astype(BF16)
    for comp in range(16):
        cols = slice(comp * chan, (comp + 1) * chan)
        val_ref[:, cols] = dot_nn(feat_ref[:, cols], vw_ref[int(comp**0.5)]).astype(BF16)
    for ref in (u_acc, k_acc, p_acc, q_src, p_src):
        ref[...] = jnp.zeros_like(ref)
    p_out[...] = jnp.zeros_like(p_out)

    small_2 = small(qrys.at[1], metas.at[1], 2, along)
    small_3a = small(qrys.at[1], metas.at[1], 3, twin)
    small_3b = small(qrys.at[2], metas.at[2], 3, twin)
    big_2 = [big(cots.at[1], 2, c, along) for c in range(CHUNKS)]
    big_3a = [big(cots.at[1], 3, c, twin) for c in range(CHUNKS)]
    big_3b = [big(cots.at[2], 3, c, twin) for c in range(CHUNKS)]

    def when_start(flag, copies):
        @pl.when(flag)
        def _():
            for item in copies:
                item.start()

    crooked = jnp.logical_not(straight)
    tables = (val_ref, key_ref, turn_ref)
    acc = (u_acc, k_acc, p_acc, q_src, p_src)
    height = 2 * TILE

    def block(first, width, own, fwd, step, cot, qry, meta, slot):
        def visit(r, carry):
            tgt = pl.ds(pl.multiple_of(r * height, height), height)
            block_terms(tables, acc, tgt, pl.ds(first, width), own, fwd, step, scale, cot, qry, meta, slot)
            return carry

        lax.fori_loop(0, atoms // height, visit, 0)

    forward = [core == 0, side == 0, side == 1, core == 1]
    steps = [1, 2, 2, 1]

    def remote(slot, first, width):
        block(
            first, width, False, forward[slot], steps[slot],
            cots.at[slot], qrys.at[slot], metas.at[slot], slot,
        )

    backs = []

    def give_back(slot, peer):
        q_out[slot] = q_src[slot].astype(BF16)
        p_out[slot, 0:8] = p_src[slot].astype(BF16)
        base = 8 + 4 * CHUNKS + 2 * slot
        pair = (
            copy(q_out.at[slot], q_back.at[slot], base, peer),
            copy(p_out.at[slot], p_back.at[slot], base + 1, peer),
        )
        begin(pair)
        backs.extend(pair)

    def arrived(copies):
        for item in copies:
            item.wait_recv()

    for first in range(0, atoms, height):
        block(first, height, True, None, 0, cot_ref, qry_ref, meta_ref, 4)
    arrived(small_1)
    begin(small_2)
    when_start(straight, small_3a)
    arrived(small_0)
    arrived(big_0)
    remote(0, 0, height)
    arrived(small_2)
    when_start(crooked, small_3b)
    for c in range(CHUNKS + 2):
        if c < CHUNKS:
            arrived([big_1[c]])
            begin([big_2[c]])
            when_start(straight, [big_3a[c]])
        if c == 0:
            for first in range(height, atoms, height):
                remote(0, first, height)
            give_back(0, twin)
        if c < CHUNKS:
            remote(1, c * rows, rows)
            if c == CHUNKS - 1:
                give_back(1, across)
        if 1 <= c <= CHUNKS:
            arrived([big_2[c - 1]])
            when_start(crooked, [big_3b[c - 1]])
            remote(2, (c - 1) * rows, rows)
            if c == CHUNKS:
                give_back(2, far)
        if c >= 2:
            if c == 2:
                arrived(small_3a)
            arrived([big_3a[c - 2]])
            remote(3, (c - 2) * rows, rows)
    give_back(3, near)
    for comp in range(1, 16):
        cols = slice(comp * chan, (comp + 1) * chan)
        out_ref[:, cols] = dot_nt(u_acc[:, cols].astype(BF16), vw_ref[int(comp**0.5)]).astype(BF16)
    total_p = p_acc[...].T[0:8] + p_src[4]
    total_q = q_src[4]
    arrived(backs)
    for slot in range(4):
        total_q = total_q + q_back[slot].astype(F32)
        total_p = total_p + p_back[slot].astype(F32)[0:8]
    mixed = dot_nt(u_acc[:, :chan].astype(BF16), vw_ref[0])
    mixed += dot_nt(total_q.astype(BF16), qw_ref[...])
    mixed += dot_nt(k_acc[...].astype(BF16), kw_ref[...])
    out_ref[:, :chan] = mixed.astype(BF16)
    force_ref[...] = -total_p[0:3]
    for item in sent:
        item.wait_send()
    for item in (*small_3a, *big_3a):
        item.wait_send()


def shards(
    features, cotangent, positions, value_weight, query_weight, key_weight, ghost_index, tile_pairs, tile_counts
):
    atoms, feat = features.shape
    width = query_weight.shape[1]
    slots = tile_pairs.shape[2]
    tiles = atoms // TILE
    gtiles = ghost_index.shape[2] // TILE
    domains = lax.axis_size("dom")

    used = jnp.arange(slots, dtype=jnp.int32)[None, :] < tile_counts[0][:, None]
    ids = jnp.arange(tiles, dtype=jnp.int32)
    hit_a = tile_pairs[0, :, :, 0, None] == ids
    hit_b = tile_pairs[0, :, :, 1, None] == ids
    active = jnp.sum(
        (hit_a[:, :, :, None] & hit_b[:, :, None, :] & used[:, :, None, None]).astype(F32), axis=1
    )
    intra = jnp.maximum(active[0], active[0].T)
    atom_ids = jnp.arange(atoms, dtype=jnp.int32)
    listed = ghost_index[0].reshape(2 * gtiles, TILE)
    ghost_rows = jnp.sum((listed[:, :, None] == atom_ids).astype(F32), axis=1)
    act_tiles = active[1:, :, :gtiles].transpose(0, 2, 1).reshape(2 * gtiles, tiles)
    one_hot = jnp.eye(tiles, dtype=F32)
    spread = lambda table: jnp.repeat(table, TILE, axis=1)
    blank = jnp.zeros((1, atoms), F32)
    points = positions.astype(F32)
    shared = [points, ghost_rows, spread(act_tiles)]
    meta = jnp.concatenate([*shared, spread(one_hot), blank], axis=0).astype(BF16)
    turn = jnp.concatenate([*shared, spread(intra), blank], axis=0).T
    vmem = pltpu.VMEM
    adjoint, forces = pl.pallas_call(
        functools.partial(layer_kernel, domains, width ** (-0.5)),
        out_shape=[
            jax.ShapeDtypeStruct((atoms, feat), BF16),
            jax.ShapeDtypeStruct((3, atoms), F32),
        ],
        in_specs=whole(7),
        out_specs=whole(2),
        scratch_shapes=[
            vmem((atoms, feat), BF16),
            vmem((atoms, width), BF16),
            vmem((atoms, width), BF16),
            vmem((4, atoms, feat), BF16),
            vmem((4, atoms, width), BF16),
            vmem((4, 16, atoms), BF16),
            vmem((atoms, feat), F32),
            vmem((atoms, width), F32),
            vmem((atoms, 128), F32),
            vmem((5, atoms, width), F32),
            vmem((5, 8, atoms), F32),
            vmem((4, atoms, width), BF16),
            vmem((4, 16, atoms), BF16),
            vmem((4, atoms, width), BF16),
            vmem((4, 16, atoms), BF16),
            pltpu.SemaphoreType.DMA((16 + 4 * CHUNKS,)),
            pltpu.SemaphoreType.DMA((16 + 4 * CHUNKS,)),
        ],
        compiler_params=pltpu.CompilerParams(
            vmem_limit_bytes=VMEM_BYTES, collective_id=0, has_side_effects=True
        ),
    )(features, cotangent, meta, turn, value_weight, query_weight, key_weight)
    return adjoint, forces


def solution(mesh):
    both = ("groups", "dom")
    placed = (
        P(both, None),
        P(both, None),
        P(None, both),
        P(),
        P(),
        P(),
        P(both, None, None),
        P(both, None, None, None),
        P(both, None),
    )
    return jax.shard_map(
        shards, mesh=mesh, in_specs=placed, out_specs=(P(both, None), P(None, both)), check_vma=False
    )
```
